512 devices in a mesh: seq: 64 (over z_lo, x, core), head: 8 (over z_hi, y).
Axes of the slice: x: 4, y: 4, z: 16 (z_hi: 2, z_lo: 8; z = z_hi * 8 + z_lo), core: 2. Of those that a mesh axis runs over, the one named last changes fastest.
Arguments:
- tokens: bfloat16 [8192, 3072], P('seq', 'head'), may hold values from -6 to 6
- qkv_weight: bfloat16 [3072, 6144], P('seq', 'head'), may hold values from -1 to 1
- qkv_bias: float32 [6144], P('head'), may hold values from -1.5 to 1.5
- q_gain: float32 [128], replicated, may hold values from 0.5 to 6.5
- k_gain: float32 [128], replicated, may hold values from 0.5 to 6.5
- cache_kv: bfloat16 [8192, 4096], P('seq', 'head'), may hold values from -127 to 127
- cache_scale: float32 [128, 16], P('seq', 'head'), may hold values from 0.008 to 0.03
- cache_code: int32 [128], P('seq'), may hold values from 0 to 1
- block_mask: int32 [128, 128], replicated, may hold values from 0 to 1, as said below
- out_weight: bfloat16 [2048, 3072], P('head', 'seq'), may hold values from -0.375 to 0.375
- out_bias: float32 [3072], P('head'), may hold values from -2.5 to 2.5
- out_gate: float32 [3072], P('head'), may hold values from -3 to 3
Outputs:
- attn_out: bfloat16 [8192, 3072], P('seq', 'head')
- block_mass: float32 [16, 128, 128], P('head', 'seq')
The draws below stay inside these ranges and needn't reach their ends.
Inputs may be any that keep to these rules, and one draw needn't show every extreme that they name: Every block attends to itself: block_mask[b, b] = 1.
All inputs are finite; a program needn't handle non-finite values.
Results may differ from the reference program's by a relative error of at most 0.019.
The reference program's roundings to bfloat16 on the way count: a program that leaves them out, or rounds other values in their place, can miss the bound.
Values may be sent and summed in bfloat16 or wider, within the bound.
No kernel may reach another device: no remote copies, remote signals or barrier semaphores. Data moves between devices by JAX's collectives and lax.ppermute only.
A program may use at most 128 MiB of HBM per device.

```python
import math
import jax
import jax.numpy as jnp
from jax import lax

D = 3072
HEADS = 16
DH = 128
BLK = 64
TOKENS = 8192
NB = 128


def draw_tokens(key, part):
    key = jax.random.fold_in(key, 11)
    first_key = jax.random.fold_in(key, 0)
    drawn = jax.random.normal(first_key, (TOKENS, D), jnp.float32)
    return jnp.clip(drawn, -6.0, 6.0).astype(jnp.bfloat16)


def draw_qkv_weight(key, part):
    key = jax.random.fold_in(key, 12)
    limit_value = 6.0 / math.sqrt(D)
    drawn = jnp.clip(jax.random.normal(key, (D, HEADS, 3, DH), jnp.float32) / math.sqrt(D), -limit_value, limit_value)
    return drawn.reshape(D, HEADS * 3 * DH).astype(jnp.bfloat16)


def draw_q_gain(key, part):
    key = jax.random.fold_in(key, 13)
    drawn = jnp.exp(jax.random.uniform(key, (DH,), jnp.float32, math.log(0.5), math.log(2.0)))
    return drawn


def draw_k_gain(key, part):
    key = jax.random.fold_in(key, 14)
    drawn = jnp.exp(jax.random.uniform(key, (DH,), jnp.float32, math.log(0.5), math.log(2.0)))
    return drawn


def draw_cache_kv(key, part):
    key = jax.random.fold_in(key, 15)
    return jax.random.randint(key, (TOKENS, HEADS * 2 * DH), -127, 128).astype(jnp.bfloat16)


def draw_block_mask(key, part):
    key = jax.random.fold_in(key, 16)
    first_key, second_key = jax.random.split(key, 2)
    row_ids = jnp.arange(NB)
    density = jax.random.randint(first_key, (NB, 1), 50, 650)
    close_by = jnp.abs(row_ids[:, None] - row_ids[None, :]) <= 2
    draw_roll = jax.random.randint(second_key, (NB, NB), 0, 1000)
    chosen = (draw_roll < density + 300 * close_by.astype(jnp.int32)) | (row_ids[:, None] == row_ids[None, :])
    return chosen.astype(jnp.int32)


def set_ends(result, own_key, smallest, high):
    place = [jax.random.randint(jax.random.fold_in(own_key, axis), (), 0, length) for axis, length in enumerate(result.shape)]
    widest = result.shape.index(max(result.shape))
    beside = place[:widest] + [(place[widest] + 1) % result.shape[widest]] + place[widest + 1:]
    return result.at[tuple(place)].set(smallest).at[tuple(beside)].set(high)


def raised(values, stream_key, source, target, shards_of, factor):
    owner, partner = [(jnp.arange(values.shape[axis_at]) // (values.shape[axis_at] // shards_of)).reshape([-1 if axis == axis_at else 1 for axis in range(values.ndim)]) for axis_at in (source, target)]
    chosen = jax.random.permutation(stream_key, shards_of)[partner]
    strong = (owner == chosen) | (owner == (partner + shards_of // 2) % shards_of)
    return jnp.where(strong, factor * values, values)


def level_of(own_key, dims, cuts, smallest, largest):
    def one(dim, blocks):
        draws = jax.random.uniform(jax.random.fold_in(jax.random.fold_in(own_key, 6), dim), (blocks,), jnp.float32, smallest / len(cuts), largest / len(cuts))
        return jnp.repeat(jnp.exp(draws), dims[dim] // blocks).reshape((-1,) + (1,) * (len(dims) - dim - 1))

    loudness = one(*cuts[0])
    for cut in cuts[1:]:
        loudness = loudness * one(*cut)
    return loudness


def gaussian(key, extent, width, most, cuts=(), held_as=jnp.bfloat16):
    gain = level_of(key, extent, cuts, -0.22, 0.18) if cuts else 1.0
    values = jax.random.normal(key, extent, jnp.float32) * width * gain
    return jnp.minimum(jnp.maximum(values, -most), most).astype(held_as)


def noise_with(own_key, dims, deviation, reach, cuts, heavy, kind=jnp.bfloat16):
    values = deviation * jax.random.normal(own_key, dims, jnp.float32)
    if cuts:
        values = values * level_of(own_key, dims, cuts, -0.22, 0.18)
    return jnp.clip(raised(values, jax.random.fold_in(own_key, 3), *heavy), -reach, reach).astype(kind)


def setup_inputs(seed: int = 0) -> dict:
    arg_keys = jax.random.split(jax.random.key(seed), 13)
    tokens = draw_tokens(jax.random.fold_in(arg_keys[12], 71), 0)
    qkv_weight = draw_qkv_weight(jax.random.fold_in(arg_keys[12], 71), 0)
    qkv_bias = gaussian(arg_keys[2], (HEADS * 3 * DH,), 0.3, 1.5, ((0, 8),), jnp.float32)
    q_gain = draw_q_gain(jax.random.fold_in(arg_keys[12], 71), 0)
    k_gain = draw_k_gain(jax.random.fold_in(arg_keys[12], 71), 0)
    cache_kv = draw_cache_kv(jax.random.fold_in(arg_keys[12], 71), 0)
    cache_scale = jnp.clip(jnp.exp(math.log(0.03) - 1.3217558 * jax.random.uniform(arg_keys[6], (NB, HEADS), jnp.float32) ** level_of(arg_keys[6], (NB, HEADS), ((0, 64), (1, 8)), -0.2, 0.2)), 0.008, 0.03)
    cache_code = set_ends(jax.random.randint(arg_keys[7], (NB,), 0, 2), jax.random.fold_in(arg_keys[7], 1), 0, 1).astype(jnp.int32)
    block_mask = draw_block_mask(jax.random.fold_in(arg_keys[12], 71), 0)
    out_weight = noise_with(arg_keys[9], (HEADS * DH, D), (HEADS * DH) ** -0.5, 0.375, ((0, 8), (1, 64)), (0, 1, 64, 4.0))
    out_bias = gaussian(arg_keys[10], (D,), 0.5, 2.5, ((0, 8),), jnp.float32)
    out_gate = gaussian(arg_keys[11], (D,), 1.0, 3.0, ((0, 8),), jnp.float32)
    return {"tokens": tokens, "qkv_weight": qkv_weight, "qkv_bias": qkv_bias, "q_gain": q_gain, "k_gain": k_gain, "cache_kv": cache_kv, "cache_scale": cache_scale, "cache_code": cache_code, "block_mask": block_mask, "out_weight": out_weight, "out_bias": out_bias, "out_gate": out_gate}


def rms_scaled(vectors, gains):
    mean_square = lax.optimization_barrier(jnp.mean(vectors * vectors, axis=-1, keepdims=True))
    return vectors * lax.rsqrt(mean_square + 1e-06) * gains

def reference(tokens, qkv_weight, qkv_bias, q_gain, k_gain, cache_kv, cache_scale, cache_code, block_mask, out_weight, out_bias, out_gate):
    token_total = tokens.shape[0]
    block_total = token_total // BLK
    query_rows = min(token_total, BLK * math.gcd(block_total, max(1, 512 // BLK)))
    projected = jnp.dot(tokens, qkv_weight, preferred_element_type=jnp.float32) + qkv_bias
    projected = projected.reshape(token_total, HEADS, 3, DH)
    queries = rms_scaled(projected[:, :, 0], q_gain).astype(jnp.bfloat16)
    fresh_keys = rms_scaled(projected[:, :, 1], k_gain).astype(jnp.bfloat16)
    fresh_values = projected[:, :, 2].astype(jnp.bfloat16)
    cached = cache_kv.reshape(token_total, HEADS, 2, DH).astype(jnp.float32)
    factor = jnp.repeat(cache_scale, BLK, axis=0)[:, :, None]
    use_cache = (jnp.repeat(cache_code, BLK) == 1)[:, None, None]
    key_rows = jnp.where(use_cache, (cached[:, :, 0] * factor).astype(jnp.bfloat16), fresh_keys)
    value_rows = jnp.where(use_cache, (cached[:, :, 1] * factor).astype(jnp.bfloat16), fresh_values)
    row_mask = jnp.repeat(block_mask, BLK, axis=0)
    inv_root = 1.0 / math.sqrt(DH)

    def one_head(head_inputs):
        head_queries, head_keys, head_values = head_inputs

        def one_block(start_row):
            block_queries = lax.dynamic_slice_in_dim(head_queries, start_row, query_rows, 0)
            mask_rows = lax.dynamic_slice_in_dim(row_mask, start_row, query_rows, 0)
            allowed = jnp.repeat(mask_rows, BLK, axis=1) == 1
            scores = jnp.dot(block_queries, head_keys.T, preferred_element_type=jnp.float32) * inv_root
            top_score = lax.optimization_barrier(jnp.max(jnp.where(allowed, scores, -jnp.inf), axis=1, keepdims=True))
            exp_scores = jnp.where(allowed, jnp.exp(scores - top_score), 0.0)
            probs = exp_scores / lax.optimization_barrier(jnp.sum(exp_scores, axis=1, keepdims=True))
            attended = jnp.dot(probs.astype(jnp.bfloat16), head_values, preferred_element_type=jnp.float32)
            mass_part = probs.reshape(query_rows // BLK, BLK, block_total, BLK).sum(axis=(1, 3))
            return (attended, mass_part)
        starts = jnp.arange(token_total // query_rows, dtype=jnp.int32) * query_rows
        attended, mass_part = lax.map(one_block, starts)
        return (attended.reshape(token_total, DH), mass_part.reshape(block_total, block_total))
    attended, block_mass = lax.map(one_head, (queries.transpose(1, 0, 2), key_rows.transpose(1, 0, 2), value_rows.transpose(1, 0, 2)))
    attended = attended.transpose(1, 0, 2).reshape(token_total, HEADS * DH).astype(jnp.bfloat16)
    summed = jnp.dot(attended, out_weight, preferred_element_type=jnp.float32)
    attn_out = ((summed + out_bias) * out_gate).astype(jnp.bfloat16)
    return (attn_out, block_mass)
```

```python
import functools
import math

import jax
import jax.numpy as jnp
from jax import lax
from jax.experimental import pallas as pl
from jax.experimental.pallas import tpu as pltpu
from jax.sharding import Mesh, PartitionSpec as P

BF = jnp.bfloat16
F32 = jnp.float32
DH = 128
FRESH = 1e30
FLOOR = -1e29
SHUT = -1e30
LOG2E = 1.4426950408889634

VM = pl.BlockSpec(memory_space=pltpu.VMEM)
SM = pl.BlockSpec(memory_space=pltpu.SMEM)


def call(kernel, outs, n_in, n_smem, scratch=(), flops=0, name=None):
    multiple = isinstance(outs, (list, tuple))
    return pl.pallas_call(
        kernel,
        out_shape=outs,
        in_specs=[SM] * n_smem + [VM] * (n_in - n_smem),
        out_specs=[VM] * len(outs) if multiple else VM,
        scratch_shapes=list(scratch),
        compiler_params=pltpu.CompilerParams(vmem_limit_bytes=48 * 1024 * 1024),
        name=name,
    )


def nt(a, b, precision=None):
    return lax.dot_general(
        a, b, (((1,), (1,)), ((), ())), preferred_element_type=F32, precision=precision
    )


def tn(a, b):
    return lax.dot_general(a, b, (((0,), (0,)), ((), ())), preferred_element_type=F32)


def prep_kernel(pos, scale, code, w_ref, cache_ref, tok_ref, ot_ref, keep_ref, send_ref, first_ref):
    zh = pos[0]
    for t in range(3):
        a = w_ref[:, t * 128 : (t + 1) * 128]
        b = w_ref[:, 384 + t * 128 : 384 + (t + 1) * 128]
        keep_ref[t * 48 : (t + 1) * 48, :] = jnp.where(zh == 0, a, b)
        send_ref[t * 48 : (t + 1) * 48, :] = jnp.where(zh == 0, b, a)
    for part in range(2):
        for blk in range(2):
            rows = slice(blk * 64, blk * 64 + 64)
            at = slice(144 + part * 128 + blk * 64, 144 + part * 128 + blk * 64 + 64)
            both = []
            for j in range(2):
                raw = cache_ref[rows, j * 256 + part * 128 : j * 256 + part * 128 + 128]
                row = (raw.astype(F32) * scale[blk, j]).astype(BF)
                both.append(jnp.where(code[blk] == 1, row, jnp.full_like(row, FRESH)))
            keep_ref[at, :] = jnp.where(zh == 0, both[0], both[1])
            send_ref[at, :] = jnp.where(zh == 0, both[1], both[0])
    for f in range(3):
        first_ref[f * 128 : (f + 1) * 128, :] = tok_ref[:, f * 128 : (f + 1) * 128]
    for j in range(2):
        first_ref[384 + j * 48 : 384 + (j + 1) * 48, :] = ot_ref[:, j * 128 : (j + 1) * 128]


def project_kernel(
    pos, x0, x1, x2, x3, wown, woth, bias, qg, kg, keep, recv, q_ref, kv_ref
):
    zh, c, y = pos[0], pos[1], pos[2]
    total = jnp.zeros((256, 384), F32)
    for k, xr in enumerate((x0, x1, x2, x3)):
        yy = lax.rem(y + (4 - k), 4)
        for w in range(2):
            slot = jnp.where(zh == 0, w, 1 - w)
            rows = []
            for z in range(2):
                rows.append(jnp.concatenate([xr[w * 2 + z, f * 128 : (f + 1) * 128, :] for f in range(3)], axis=1))
            x = jnp.concatenate(rows, axis=0)
            pieces = []
            for xx in range(4):
                own = jnp.concatenate([wown[xx, yy, slot, t * 48 : (t + 1) * 48, :] for t in range(3)], axis=1)
                oth = jnp.concatenate([woth[xx, yy, slot, t * 48 : (t + 1) * 48, :] for t in range(3)], axis=1)
                pieces.append(jnp.where(c == 0, own, oth))
                pieces.append(jnp.where(c == 0, oth, own))
            total = total + jnp.dot(x, jnp.concatenate(pieces, axis=0), preferred_element_type=F32)
    total = total + jnp.where(zh == 0, bias[:, :384], bias[:, 384:])

    def scaled(v, gain):
        ms = jnp.mean(v * v, axis=-1, keepdims=True)
        return (v * lax.rsqrt(ms + 1e-06) * gain).astype(BF)

    q_ref[...] = scaled(total[:, :128], qg[...])
    fresh = (scaled(total[:, 128:256], kg[...]), total[:, 256:].astype(BF))
    for part in range(2):
        at = slice(144 + part * 128, 144 + part * 128 + 128)
        a, b = keep[at, :], recv[at, :]
        for z in range(2):
            cached = jnp.where(zh == z, a, b)
            new = fresh[part][z * 128 : (z + 1) * 128]
            kv_ref[part * 256 + z * 128 : part * 256 + (z + 1) * 128, :] = jnp.where(
                cached.astype(F32) < 1e29, cached, new
            )


def attend_kernel(q_ref, kv0, kv1, mask_ref, out_ref, s_ref):
    unit = LOG2E / math.sqrt(DH)
    q = jnp.concatenate([q_ref[i] for i in range(4)], axis=0)
    top = jnp.full((1, 1024), FLOOR, F32)
    for ch in range(8):
        kv = (kv0, kv1)[ch // 4]
        s = nt(kv[ch % 4, :256, :], q) * unit
        for b in range(4):
            row = ch * 4 + b
            open_ = mask_ref[row : row + 1, :] > 0
            sb = jnp.where(open_, s[b * 64 : (b + 1) * 64], SHUT)
            s_ref[ch * 256 + b * 64 : ch * 256 + (b + 1) * 64, :] = sb
            top = jnp.maximum(top, jnp.max(sb, axis=0, keepdims=True))
    total = jnp.zeros((1, 1024), F32)
    out = jnp.zeros((128, 1024), F32)
    mass = []
    for ch in range(8):
        kv = (kv0, kv1)[ch // 4]
        p = jnp.exp2(s_ref[ch * 256 : (ch + 1) * 256, :] - top)
        for b in range(4):
            row = jnp.sum(p[b * 64 : (b + 1) * 64], axis=0, keepdims=True)
            mass.append(row)
            total = total + row
        out = out + tn(kv[ch % 4, 256:, :], p.astype(BF))
    for i in range(4):
        cols = slice(i * 256, (i + 1) * 256)
        out_ref[i, :128, :] = out[:, cols]
        for r in range(32):
            out_ref[i, 128 + r : 129 + r, :] = mass[r][:, cols]
        out_ref[i, 160:161, :] = top[:, cols]
        out_ref[i, 161:162, :] = total[:, cols]
        out_ref[i, 162:168, :] = jnp.zeros((6, 256), F32)


def merge_kernel(pos, parts, out_ref):
    c = pos[1]
    hi = lax.Precision.HIGHEST
    tops = [parts[i, 160:161, :] for i in range(4)]
    top = jnp.maximum(jnp.maximum(tops[0], tops[1]), jnp.maximum(tops[2], tops[3]))
    factors = [jnp.exp2(t - top) for t in tops]
    total = sum(f * parts[i, 161:162, :] for i, f in enumerate(factors))
    shares = [f / total for f in factors]
    out = sum(s * parts[i, :128, :] for i, s in enumerate(shares))
    att = out.T.astype(BF)
    mass = jnp.concatenate([s * parts[i, 128:160, :] for i, s in enumerate(shares)], axis=0)
    i = lax.broadcasted_iota(jnp.int32, (128, 128), 0)
    b = lax.broadcasted_iota(jnp.int32, (128, 128), 1)
    cc = jnp.bitwise_xor((i >> 4) & 1, c)
    place = ((i >> 1) & 1) * 64 + ((i >> 2) & 3) * 16 + (i >> 5) * 4 + cc * 2 + (i & 1)
    order = (place == b).astype(F32)
    r = lax.broadcasted_iota(jnp.int32, (16, 256), 0)
    t = lax.broadcasted_iota(jnp.int32, (16, 256), 1)
    row = lax.broadcasted_iota(jnp.int32, (16, 128), 0)
    for z in range(2):
        pick = ((r < 6) & ((t >> 6) == z * 2 + (r & 1))).astype(F32)
        m = jnp.dot(nt(pick, mass, hi), order, preferred_element_type=F32, precision=hi)
        a = m.astype(BF).astype(F32)
        d = (m - a).astype(BF).astype(F32)
        e = m - a - d
        packed = jnp.where(row < 2, a, jnp.where(row < 4, d, jnp.where(row < 6, e, 0.0))).astype(BF)
        for w in range(2):
            out_ref[w * 2 + z, :128, :] = att[z * 128 : (z + 1) * 128]
            out_ref[w * 2 + z, 128:144, :] = packed


def finish_kernel(pos, att, got, oown, ooth, bias, gate, out_ref, mass_ref):
    c, w = pos[1], pos[3]
    cols, weights = [], []
    for y in range(4):
        for ww in range(2):
            for j in range(2):
                cols.append(att[y, ww * 2 + j])
    a = jnp.concatenate(cols, axis=1)
    for x in range(4):
        own = jnp.concatenate(
            [oown[x, y, ww, j * 48 : (j + 1) * 48, :] for y in range(4) for ww in range(2) for j in range(2)], axis=1
        )
        oth = jnp.concatenate(
            [ooth[x, y, ww, j * 48 : (j + 1) * 48, :] for y in range(4) for ww in range(2) for j in range(2)], axis=1
        )
        weights.append(jnp.where(c == 0, own, oth))
        weights.append(jnp.where(c == 0, oth, own))
    total = nt(a, jnp.concatenate(weights, axis=0))
    out_ref[...] = ((total + bias[...]) * gate[...]).astype(BF)
    for j in range(2):
        r = got[w * 2 + j, 128:144, :].astype(F32)
        mass_ref[j] = r[0:2] + r[2:4] + r[4:6]


def swap(v, axis):
    return lax.ppermute(v, axis, [(0, 1), (1, 0)])


def turn(v, axis, k):
    return lax.ppermute(v, axis, [(i, (i + k) % 4) for i in range(4)])


def per_device(
    tokens, qkv_weight, qkv_bias, q_gain, k_gain, cache_kv, cache_scale, cache_code, block_mask, out_weight,
    out_bias, out_gate,
):
    zh, zl, x, c, w, y = (lax.axis_index(n) for n in ("zh", "zl", "x", "c", "w", "y"))
    pos = jnp.stack([zh, c, y, w]).astype(jnp.int32)
    sd = jax.ShapeDtypeStruct

    keep, send, first = call(
        prep_kernel, [sd((400, 128), BF), sd((400, 128), BF), sd((480, 128), BF)], 7, 3, name="prep"
    )(pos, cache_scale, cache_code, qkv_weight, cache_kv, tokens, out_weight.T)

    recv = swap(send, "zh")
    spread = lax.all_gather(first, ("w", "zh"), axis=0, tiled=False)
    toks = spread[:, :384]
    outs = lax.dynamic_index_in_dim(spread[:, 384:].reshape(2, 2, 96, 128), w, 1, keepdims=False)
    second = jnp.concatenate([keep[:144], recv[:144], outs.reshape(192, 128)], axis=0)
    along = lax.all_gather(second, "zl", axis=0, tiled=False)
    x1, x2, x3 = (turn(toks, "y", k) for k in (1, 2, 3))
    wts = along[:, :288].reshape(4, 2, 144, 128)
    wa = lax.all_gather(wts[:2], "x", axis=0, tiled=False)
    wb = lax.all_gather(wts[2:], "x", axis=0, tiled=False)
    wown = jnp.concatenate([wa, wb], axis=1)
    woth = swap(wown, "c")
    ow = lax.all_to_all(along[:, 288:], "y", 0, 0, tiled=True)

    q, kv = call(
        project_kernel, [sd((256, 128), BF), sd((512, 128), BF)], 12, 1, name="project"
    )(pos, toks, x1, x2, x3, wown, woth, qkv_bias[None], q_gain[None], k_gain[None], keep, recv)

    kv0 = lax.all_gather(kv, "zl", axis=0, tiled=False)
    kv1 = swap(kv0, "c")
    qs = lax.all_to_all(jnp.broadcast_to(q[None], (4, 256, 128)), "x", 0, 0, tiled=True)

    bm = block_mask.reshape(2, 4, 4, 2, 2, 2, 4, 4, 2, 2)
    zero = jnp.zeros((), jnp.int32)
    bm = lax.dynamic_slice(
        bm, (zero, zl, zero, c, zero, zero, zero, x, zero, zero), (2, 1, 4, 1, 2, 2, 4, 1, 2, 2)
    ).reshape(2, 4, 2, 2, 4, 2, 2)
    bm = jnp.where(c == 0, bm, bm[:, :, :, :, :, ::-1])
    bm = bm.transpose(5, 4, 3, 6, 1, 0, 2).reshape(32, 16)
    mask = jnp.repeat(bm.astype(F32), 64, axis=1)

    parts = call(
        attend_kernel, sd((4, 168, 256), F32), 4, 0, [pltpu.VMEM((2048, 1024), F32)], name="attend"
    )(qs, kv0, kv1, mask)
    parts = lax.all_to_all(parts, "x", 0, 0, tiled=True)
    done = call(merge_kernel, sd((4, 144, 128), BF), 2, 1, name="merge")(pos, parts)
    got = lax.all_to_all(done, ("w", "zh"), 0, 0, tiled=True)
    att = lax.all_gather(got[:, :128], "y", axis=0, tiled=False)

    oown = lax.all_gather(ow.reshape(4, 2, 96, 128), "x", axis=0, tiled=False)
    ooth = swap(oown, "c")
    return call(
        finish_kernel, [sd((128, 384), BF), sd((2, 2, 128), F32)], 7, 1, name="finish"
    )(pos, att, got, oown, ooth, out_bias[None], out_gate[None])


def solution(mesh):
    split = Mesh(mesh.devices.reshape(2, 4, 4, 2, 2, 4), ("zh", "zl", "x", "c", "w", "y"))
    seq, head = ("zh", "zl", "x", "c"), ("w", "y")
    in_specs = (
        P(seq, head), P(seq, head), P(head), P(), P(), P(seq, head), P(seq, head), P(seq), P(), P(head, seq),
        P(head), P(head),
    )
    out_specs = (P(seq, head), P(head, seq, None))
    return jax.shard_map(per_device, mesh=split, in_specs=in_specs, out_specs=out_specs, check_vma=False)
```

```python
import functools
import math

import jax
import jax.numpy as jnp
from jax import lax
from jax.experimental import pallas as pl
from jax.experimental.pallas import tpu as pltpu
from jax.sharding import Mesh, PartitionSpec as P

BF = jnp.bfloat16
F32 = jnp.float32
DH = 128
FRESH = 1e30
FLOOR = -1e29
SHUT = -1e30
LOG2E = 1.4426950408889634

VM = pl.BlockSpec(memory_space=pltpu.VMEM)
HB = pl.BlockSpec(memory_space=pltpu.HBM)


def call(kernel, outs, n_in, scratch=(), place=VM, limit=48, name=None, cover=0):
    multiple = isinstance(outs, (list, tuple))
    cost = pl.CostEstimate(flops=cover * 10**9, bytes_accessed=0, transcendentals=0) if cover else None
    return pl.pallas_call(
        kernel,
        out_shape=outs,
        in_specs=[place] * n_in,
        out_specs=[VM] * len(outs) if multiple else VM,
        scratch_shapes=list(scratch),
        compiler_params=pltpu.CompilerParams(vmem_limit_bytes=limit * 1024 * 1024 if limit else None),
        cost_estimate=cost,
        name=name,
    )


def nt(a, b, precision=None):
    return lax.dot_general(
        a, b, (((1,), (1,)), ((), ())), preferred_element_type=F32, precision=precision
    )


def tn(a, b):
    return lax.dot_general(a, b, (((0,), (0,)), ((), ())), preferred_element_type=F32)


def prep_kernel(
    scale_h, code_h, w_h, cache_h, tok_h, ot_h, keep_ref, send_ref, kept_ref, sent_ref, first_ref, flip_ref, scale, code,
    w_ref, cache_ref, tok_ref, ot_ref, sems
):
    zh = lax.axis_index("zh")
    pairs = ((w_h, w_ref), (cache_h, cache_ref), (scale_h, scale), (code_h, code), (tok_h, tok_ref), (ot_h, ot_ref))
    copies = [pltpu.make_async_copy(src, dst, sems.at[i]) for i, (src, dst) in enumerate(pairs)]
    for copy in copies:
        copy.start()
    for copy in copies:
        copy.wait()
    for t in range(3):
        a = w_ref[:, t * 128 : (t + 1) * 128]
        b = w_ref[:, 384 + t * 128 : 384 + (t + 1) * 128]
        keep_ref[t * 48 : (t + 1) * 48, :] = jnp.where(zh == 0, a, b)
        send_ref[t * 48 : (t + 1) * 48, :] = jnp.where(zh == 0, b, a)
    for part in range(2):
        for blk in range(2):
            rows = slice(blk * 64, blk * 64 + 64)
            at = slice(part * 128 + blk * 64, part * 128 + blk * 64 + 64)
            cached = jnp.broadcast_to(code[0:1, blk : blk + 1], (64, 128)) == 1
            both = []
            for j in range(2):
                raw = cache_ref[rows, j * 256 + part * 128 : j * 256 + part * 128 + 128]
                factor = jnp.broadcast_to(scale[blk : blk + 1, j : j + 1], (64, 128))
                both.append(jnp.where(cached, raw.astype(F32) * factor, FRESH).astype(BF))
            kept_ref[at, :] = jnp.where(zh == 0, both[0], both[1])
            sent_ref[at, :] = jnp.where(zh == 0, both[1], both[0])
    for f in range(3):
        first_ref[f * 128 : (f + 1) * 128, :] = tok_ref[:, f * 128 : (f + 1) * 128]
    for j in range(2):
        flip_ref[j * 48 : (j + 1) * 48, :] = ot_ref[:, j * 128 : (j + 1) * 128]


def projected(xa, xb, wown, woth):
    zh, c = lax.axis_index("zh"), lax.axis_index("c")
    total = jnp.zeros((256, 384), F32)
    for yy in range(4):
        for w in range(2):
            slot = jnp.where(zh == 0, w, 1 - w)
            rows = []
            for z in range(2):
                rows.append(jnp.concatenate([(xa, xb)[w][yy, z, f * 128 : (f + 1) * 128, :] for f in range(3)], axis=1))
            x = jnp.concatenate(rows, axis=0)
            pieces = []
            for xx in range(4):
                own = jnp.concatenate([wown[xx, yy, slot, t * 48 : (t + 1) * 48, :] for t in range(3)], axis=1)
                oth = jnp.concatenate([woth[xx, yy, slot, t * 48 : (t + 1) * 48, :] for t in range(3)], axis=1)
                pieces.append(jnp.where(c == 0, own, oth))
                pieces.append(jnp.where(c == 0, oth, own))
            total = total + jnp.dot(x, jnp.concatenate(pieces, axis=0), preferred_element_type=F32)
    return total


def scaled(v, gain):
    ms = jnp.mean(v * v, axis=-1, keepdims=True)
    return (v * lax.rsqrt(ms + 1e-06) * gain).astype(BF)


def project_kernel(xa, xb, wown, woth, bias, qg, kg, mine, theirs, out_ref, kv_ref):
    zh = lax.axis_index("zh")
    total = projected(xa, xb, wown, woth) + jnp.where(zh == 0, bias[:, :384], bias[:, 384:])
    q = scaled(total[:, :128], qg[...])
    for i in range(4):
        out_ref[i, :256, :] = q
        for z in range(4):
            out_ref[i, 256 + z * 192 : 352 + z * 192, :] = mine[z * 96 : (z + 1) * 96, :]
            out_ref[i, 352 + z * 192 : 448 + z * 192, :] = theirs[z * 96 : (z + 1) * 96, :]
    kv_ref[:256, :] = scaled(total[:, 128:256], kg[...])
    kv_ref[256:, :] = total[:, 256:].astype(BF)


def select_kernel(fresh, kept, theirs, kv_ref):
    zh = lax.axis_index("zh")
    for part in range(2):
        a = kept[part * 128 : part * 128 + 128, :]
        b = theirs[384 + part * 128 : 384 + part * 128 + 128, :]
        for z in range(2):
            rows = slice(part * 256 + z * 128, part * 256 + (z + 1) * 128)
            cached = jnp.where(zh == z, a, b)
            kv_ref[rows, :] = jnp.where(cached.astype(F32) < 1e29, cached, fresh[rows, :])


def attend_kernel(q_ref, kv0, kv1, bm_ref, out_ref, s_ref, mask_ref):
    unit = LOG2E / math.sqrt(DH)
    zl, x, c = (lax.axis_index(n) for n in ("zl", "x", "c"))
    r = lax.broadcasted_iota(jnp.int32, (32, 128), 0)
    b = lax.broadcasted_iota(jnp.int32, (32, 128), 1)
    cc = jnp.bitwise_xor(r >> 4, c)
    keys = ((r >> 1) & 1) * 64 + ((r >> 2) & 3) * 16 + x * 4 + cc * 2 + (r & 1)
    picked = nt((keys == b).astype(BF), bm_ref[...].astype(F32).astype(BF))
    a = lax.broadcasted_iota(jnp.int32, (128, 1024), 0)
    t = lax.broadcasted_iota(jnp.int32, (128, 1024), 1)
    rows = ((t >> 7) & 1) * 64 + zl * 16 + (t >> 8) * 4 + c * 2 + ((t >> 6) & 1)
    mask_ref[...] = jnp.dot(picked.astype(BF), (rows == a).astype(BF), preferred_element_type=F32)
    q = jnp.concatenate([q_ref[i, :256, :] for i in range(4)], axis=0)
    top = jnp.full((1, 1024), FLOOR, F32)
    for ch in range(8):
        kv = (kv0, kv1)[ch // 4]
        s = nt(kv[ch % 4, :256, :], q) * unit
        for b in range(4):
            row = ch * 4 + b
            open_ = mask_ref[row : row + 1, :] > 0.5
            sb = jnp.where(open_, s[b * 64 : (b + 1) * 64], SHUT)
            s_ref[ch * 256 + b * 64 : ch * 256 + (b + 1) * 64, :] = sb
            top = jnp.maximum(top, jnp.max(sb, axis=0, keepdims=True))
    total = jnp.zeros((1, 1024), F32)
    out = jnp.zeros((128, 1024), F32)
    mass = []
    for ch in range(8):
        kv = (kv0, kv1)[ch // 4]
        p = jnp.exp2(s_ref[ch * 256 : (ch + 1) * 256, :] - top)
        for b in range(4):
            row = jnp.sum(p[b * 64 : (b + 1) * 64], axis=0, keepdims=True)
            mass.append(row)
            total = total + row
        out = out + tn(kv[ch % 4, 256:, :], p.astype(BF))
    for i in range(4):
        cols = slice(i * 256, (i + 1) * 256)
        out_ref[i, :128, :] = out[:, cols]
        for r in range(32):
            out_ref[i, 128 + r : 129 + r, :] = mass[r][:, cols]
        out_ref[i, 160:161, :] = top[:, cols]
        out_ref[i, 161:162, :] = total[:, cols]
        out_ref[i, 162:168, :] = jnp.zeros((6, 256), F32)


def merge_kernel(parts, out_ref):
    c = lax.axis_index("c")
    hi = lax.Precision.HIGHEST
    tops = [parts[i, 160:161, :] for i in range(4)]
    top = jnp.maximum(jnp.maximum(tops[0], tops[1]), jnp.maximum(tops[2], tops[3]))
    factors = [jnp.exp2(t - top) for t in tops]
    total = sum(f * parts[i, 161:162, :] for i, f in enumerate(factors))
    shares = [f / total for f in factors]
    out = sum(s * parts[i, :128, :] for i, s in enumerate(shares))
    att = out.T.astype(BF)
    mass = jnp.concatenate([s * parts[i, 128:160, :] for i, s in enumerate(shares)], axis=0)
    i = lax.broadcasted_iota(jnp.int32, (128, 128), 0)
    b = lax.broadcasted_iota(jnp.int32, (128, 128), 1)
    cc = jnp.bitwise_xor((i >> 4) & 1, c)
    place = ((i >> 1) & 1) * 64 + ((i >> 2) & 3) * 16 + (i >> 5) * 4 + cc * 2 + (i & 1)
    order = (place == b).astype(F32)
    r = lax.broadcasted_iota(jnp.int32, (16, 256), 0)
    t = lax.broadcasted_iota(jnp.int32, (16, 256), 1)
    row = lax.broadcasted_iota(jnp.int32, (16, 128), 0)
    pick = ((r < 12) & ((t >> 6) == (r & 3))).astype(F32)
    m = jnp.dot(nt(pick, mass, hi), order, preferred_element_type=F32, precision=hi)
    a = m.astype(BF).astype(F32)
    d = (m - a).astype(BF).astype(F32)
    e = m - a - d
    packed = jnp.where(row < 4, a, jnp.where(row < 8, d, jnp.where(row < 12, e, 0.0))).astype(BF)
    out_ref[:256, :] = att
    out_ref[256:272, :] = packed


def finish_kernel(att, rows, oown, ooth, bias, gate, out_ref, mass_ref):
    zh, c, w = (lax.axis_index(n) for n in ("zh", "c", "w"))
    a = jnp.concatenate([att[y, i] for y in range(4) for i in range(4)], axis=1)
    weights = []
    for x in range(4):
        both = []
        for ref in (oown, ooth):
            piece = []
            for y in range(4):
                for ww in range(2):
                    slot = jnp.where(zh == 0, ww, 1 - ww)
                    for j in range(2):
                        start = pl.multiple_of(256 + y * 192 + slot * 96 + j * 48, 16)
                        piece.append(ref[x, pl.ds(start, 48), :])
            both.append(jnp.concatenate(piece, axis=1))
        weights.append(jnp.where(c == 0, both[0], both[1]))
        weights.append(jnp.where(c == 0, both[1], both[0]))
    total = nt(a, jnp.concatenate(weights, axis=0))
    out_ref[...] = ((total + bias[...]) * gate[...]).astype(BF)
    for j in range(2):
        r = rows[w * 2 + j, 256:272, :].astype(F32)
        lower = r[0:2] + r[4:6] + r[8:10]
        upper = r[2:4] + r[6:8] + r[10:12]
        mass_ref[j] = jnp.where(zh == 0, lower, upper)


def swap(v, axis):
    return lax.ppermute(v, axis, [(0, 1), (1, 0)])


def spread(v, axis):
    wide = jnp.broadcast_to(v[None], (4,) + v.shape)
    return lax.all_to_all(wide, axis, 0, 0, tiled=True)


def turn(v, axis, k):
    return lax.ppermute(v, axis, [(i, (i + k) % 4) for i in range(4)])


def per_device(
    tokens, qkv_weight, qkv_bias, q_gain, k_gain, cache_kv, cache_scale, cache_code, block_mask, out_weight,
    out_bias, out_gate,
):
    sd = jax.ShapeDtypeStruct

    keep, send, kept, sent, first, flip = call(
        prep_kernel,
        [sd((144, 128), BF)] * 2 + [sd((256, 128), BF)] * 2 + [sd((384, 128), BF), sd((96, 128), BF)],
        6,
        [
            pltpu.VMEM((2, 2), F32), pltpu.VMEM((1, 2), jnp.int32), pltpu.VMEM((48, 768), BF),
            pltpu.VMEM((128, 512), BF), pltpu.VMEM((128, 384), BF), pltpu.VMEM((48, 256), BF),
            pltpu.SemaphoreType.DMA((6,)),
        ],
        HB, None, "prep",
    )(cache_scale, cache_code.reshape(1, 2), qkv_weight, cache_kv, tokens, out_weight.T)

    recv = swap(send, "zh")
    flip = lax.ppermute(
        flip, ("zh", "zl", "w", "y"),
        [
            (((zh * 4 + zl) * 2 + w) * 4 + y, ((w * 4 + y) * 2 + zh) * 4 + zl)
            for zh in range(2) for zl in range(4) for w in range(2) for y in range(4)
        ],
    )
    pay, first = lax.optimization_barrier((jnp.concatenate([keep, recv, flip], axis=0), first))
    along = spread(pay, "zl").reshape(4, 384, 128)
    toks = lax.all_gather(first, ("w", "zh"), axis=0, tiled=False)
    along, toks = lax.optimization_barrier((along, toks))
    wown = spread(along[:, :288], "x")
    xa = lax.all_gather(toks[:2], "y", axis=0, tiled=False)
    wown, xa, last = lax.optimization_barrier((wown, xa, toks[2:]))
    woth = swap(wown, "c")
    mine = jnp.concatenate([along[:, 288:].reshape(384, 128), sent], axis=0)
    theirs = swap(mine, "zh")
    xb = lax.all_gather(last, "y", axis=0, tiled=False)
    woth, theirs, xb = lax.optimization_barrier((woth, theirs, xb))
    woth = woth.reshape(4, 4, 2, 144, 128)
    wown = wown.reshape(4, 4, 2, 144, 128)

    q, fresh = call(project_kernel, [sd((4, 1024, 128), BF), sd((512, 128), BF)], 9, limit=24, name="project")(
        xa, xb, wown, woth, qkv_bias[None], q_gain[None], k_gain[None], mine, theirs
    )
    qs = lax.all_to_all(q, "x", 0, 0, tiled=True)
    kv = call(select_kernel, sd((512, 128), BF), 3, limit=24, name="select", cover=30)(fresh, kept, theirs)
    kv0 = lax.all_gather(kv, "zl", axis=0, tiled=False)
    kv1 = swap(kv0, "c")

    parts = call(
        attend_kernel, sd((4, 168, 256), F32), 4, [pltpu.VMEM((2048, 1024), F32), pltpu.VMEM((32, 1024), F32)],
        limit=32, name="attend",
    )(qs, kv0, kv1, block_mask)
    late, parts = lax.optimization_barrier((qs, parts))
    parts = lax.all_to_all(parts, "x", 0, 0, tiled=True)
    ooth = swap(late, "c")
    parts, ooth = lax.optimization_barrier((parts, ooth))
    done = call(merge_kernel, sd((272, 128), BF), 1, limit=16, name="merge")(parts)
    rows = lax.all_gather(done, ("w", "zh"), axis=0, tiled=False)
    att = lax.all_gather(
        lax.dynamic_slice_in_dim(rows, lax.axis_index("zh") * 128, 128, 1), "y", axis=0, tiled=False
    )
    return call(finish_kernel, [sd((128, 384), BF), sd((2, 2, 128), F32)], 6, limit=24, name="finish")(
        att, rows, qs, ooth, out_bias[None], out_gate[None]
    )


def solution(mesh):
    split = Mesh(mesh.devices.reshape(2, 4, 4, 2, 2, 4), ("zh", "zl", "x", "c", "w", "y"))
    seq, head = ("zh", "zl", "x", "c"), ("w", "y")
    in_specs = (
        P(seq, head), P(seq, head), P(head), P(), P(), P(seq, head), P(seq, head), P(seq), P(), P(head, seq),
        P(head), P(head),
    )
    out_specs = (P(seq, head), P(head, seq, None))
    return jax.shard_map(per_device, mesh=split, in_specs=in_specs, out_specs=out_specs, check_vma=False)
```

```python
import functools
import math

import jax
import jax.numpy as jnp
from jax import lax
from jax.experimental import pallas as pl
from jax.experimental.pallas import tpu as pltpu
from jax.sharding import Mesh, PartitionSpec as P

BF = jnp.bfloat16
F32 = jnp.float32
DH = 128
FRESH = 1e30
FLOOR = -1e29
SHUT = -1e30
LOG2E = 1.4426950408889634

VM = pl.BlockSpec(memory_space=pltpu.VMEM)
HB = pl.BlockSpec(memory_space=pltpu.HBM)


def call(kernel, outs, n_in, scratch=(), place=VM, limit=48, name=None, cover=0):
    multiple = isinstance(outs, (list, tuple))
    cost = pl.CostEstimate(flops=cover * 10**9, bytes_accessed=0, transcendentals=0) if cover else None
    return pl.pallas_call(
        kernel,
        out_shape=outs,
        in_specs=[place] * n_in,
        out_specs=[VM] * len(outs) if multiple else VM,
        scratch_shapes=list(scratch),
        compiler_params=pltpu.CompilerParams(vmem_limit_bytes=limit * 1024 * 1024 if limit else None),
        cost_estimate=cost,
        name=name,
    )


def nt(a, b, precision=None):
    return lax.dot_general(
        a, b, (((1,), (1,)), ((), ())), preferred_element_type=F32, precision=precision
    )


def tn(a, b):
    return lax.dot_general(a, b, (((0,), (0,)), ((), ())), preferred_element_type=F32)


def prep_kernel(
    scale_h, code_h, w_h, cache_h, tok_h, ot_h, keep_ref, send_ref, kept_ref, sent_ref, first_ref, flip_ref, scale, code,
    w_ref, cache_ref, tok_ref, ot_ref, sems
):
    zh = lax.axis_index("zh")
    pairs = ((w_h, w_ref), (cache_h, cache_ref), (scale_h, scale), (code_h, code), (tok_h, tok_ref), (ot_h, ot_ref))
    copies = [pltpu.make_async_copy(src, dst, sems.at[i]) for i, (src, dst) in enumerate(pairs)]
    for copy in copies:
        copy.start()
    for copy in copies:
        copy.wait()
    for t in range(3):
        a = w_ref[:, t * 128 : (t + 1) * 128]
        b = w_ref[:, 384 + t * 128 : 384 + (t + 1) * 128]
        keep_ref[t * 48 : (t + 1) * 48, :] = jnp.where(zh == 0, a, b)
        send_ref[t * 48 : (t + 1) * 48, :] = jnp.where(zh == 0, b, a)
    for part in range(2):
        for blk in range(2):
            rows = slice(blk * 64, blk * 64 + 64)
            at = slice(part * 128 + blk * 64, part * 128 + blk * 64 + 64)
            cached = jnp.broadcast_to(code[0:1, blk : blk + 1], (64, 128)) == 1
            both = []
            for j in range(2):
                raw = cache_ref[rows, j * 256 + part * 128 : j * 256 + part * 128 + 128]
                factor = jnp.broadcast_to(scale[blk : blk + 1, j : j + 1], (64, 128))
                both.append(jnp.where(cached, raw.astype(F32) * factor, FRESH).astype(BF))
            kept_ref[at, :] = jnp.where(zh == 0, both[0], both[1])
            sent_ref[at, :] = jnp.where(zh == 0, both[1], both[0])
    for f in range(3):
        first_ref[f * 128 : (f + 1) * 128, :] = tok_ref[:, f * 128 : (f + 1) * 128]
    for j in range(2):
        flip_ref[j * 48 : (j + 1) * 48, :] = ot_ref[:, j * 128 : (j + 1) * 128]


def projected(xs, wown, woth):
    zh, x0, c = (lax.axis_index(n) for n in ("zh", "x", "c"))
    total = jnp.zeros((256, 384), F32)
    for yy in range(4):
        for w in range(2):
            slot = jnp.where(zh == 0, w, 1 - w)
            rows = []
            for z in range(2):
                tiles = [xs[yy, w * 2 + z, f * 128 : (f + 1) * 128, :] for f in range(3)]
                rows.append(jnp.concatenate(tiles, axis=1))
            x = jnp.concatenate(rows, axis=0)
            pieces = []
            for xx in range(4):
                k = (x0 - xx) & 3
                own = jnp.concatenate([wown[k, yy, slot, t * 48 : (t + 1) * 48, :] for t in range(3)], axis=1)
                oth = jnp.concatenate([woth[k, yy, slot, t * 48 : (t + 1) * 48, :] for t in range(3)], axis=1)
                pieces.append(jnp.where(c == 0, own, oth))
                pieces.append(jnp.where(c == 0, oth, own))
            total = total + jnp.dot(x, jnp.concatenate(pieces, axis=0), preferred_element_type=F32)
    return total


def scaled(v, gain):
    ms = jnp.mean(v * v, axis=-1, keepdims=True)
    return (v * lax.rsqrt(ms + 1e-06) * gain).astype(BF)


def project_kernel(xs, wown, woth, bias, qg, kg, mine, theirs, out_ref, kv_ref):
    zh = lax.axis_index("zh")
    total = projected(xs, wown, woth) + jnp.where(zh == 0, bias[:, :384], bias[:, 384:])
    q = scaled(total[:, :128], qg[...])
    for i in range(4):
        out_ref[i, :256, :] = q
        for z in range(4):
            out_ref[i, 256 + z * 192 : 352 + z * 192, :] = mine[z * 96 : (z + 1) * 96, :]
            out_ref[i, 352 + z * 192 : 448 + z * 192, :] = theirs[z * 96 : (z + 1) * 96, :]
    kv_ref[:256, :] = scaled(total[:, 128:256], kg[...])
    kv_ref[256:, :] = total[:, 256:].astype(BF)


def select_kernel(fresh, kept, theirs, kv_ref):
    zh = lax.axis_index("zh")
    for part in range(2):
        a = kept[part * 128 : part * 128 + 128, :]
        b = theirs[384 + part * 128 : 384 + part * 128 + 128, :]
        for z in range(2):
            rows = slice(part * 256 + z * 128, part * 256 + (z + 1) * 128)
            cached = jnp.where(zh == z, a, b)
            kv_ref[rows, :] = jnp.where(cached.astype(F32) < 1e29, cached, fresh[rows, :])


def thirds(v):
    a = v.astype(BF).astype(F32)
    b = (v - a).astype(BF).astype(F32)
    return a, b, v - a - b


def attend_kernel(q_ref, kv0, kv1, bm_ref, out_ref, s_ref, mask_ref):
    unit = LOG2E / math.sqrt(DH)
    zl, x, c = (lax.axis_index(n) for n in ("zl", "x", "c"))
    r = lax.broadcasted_iota(jnp.int32, (32, 128), 0)
    b = lax.broadcasted_iota(jnp.int32, (32, 128), 1)
    cc = jnp.bitwise_xor(r >> 4, c)
    keys = ((r >> 1) & 1) * 64 + ((r >> 2) & 3) * 16 + x * 4 + cc * 2 + (r & 1)
    picked = nt((keys == b).astype(BF), bm_ref[...].astype(F32).astype(BF))
    a = lax.broadcasted_iota(jnp.int32, (128, 1024), 0)
    t = lax.broadcasted_iota(jnp.int32, (128, 1024), 1)
    rows = ((t >> 7) & 1) * 64 + zl * 16 + (t >> 8) * 4 + c * 2 + ((t >> 6) & 1)
    mask_ref[...] = jnp.dot(picked.astype(BF), (rows == a).astype(BF), preferred_element_type=F32)
    q = jnp.concatenate([q_ref[i, :256, :] for i in range(4)], axis=0)
    top = jnp.full((1, 1024), FLOOR, F32)
    for ch in range(8):
        kv = (kv0, kv1)[ch // 4]
        s = nt(kv[ch % 4, :256, :], q) * unit
        for b in range(4):
            row = ch * 4 + b
            open_ = mask_ref[row : row + 1, :] > 0.5
            sb = jnp.where(open_, s[b * 64 : (b + 1) * 64], SHUT)
            s_ref[ch * 256 + b * 64 : ch * 256 + (b + 1) * 64, :] = sb
            top = jnp.maximum(top, jnp.max(sb, axis=0, keepdims=True))
    total = jnp.zeros((1, 1024), F32)
    out = jnp.zeros((128, 1024), F32)
    mass = []
    for ch in range(8):
        kv = (kv0, kv1)[ch // 4]
        p = jnp.exp2(s_ref[ch * 256 : (ch + 1) * 256, :] - top)
        for b in range(4):
            row = jnp.sum(p[b * 64 : (b + 1) * 64], axis=0, keepdims=True)
            mass.append(row)
            total = total + row
        out = out + tn(kv[ch % 4, 256:, :], p.astype(BF))
    sums = jnp.concatenate(mass, axis=0)
    high = sums.astype(BF)
    low = (sums - high.astype(F32)).astype(BF)
    rest = jnp.concatenate([*thirds(top), *thirds(total), jnp.zeros((10, 1024), F32)], axis=0).astype(BF)
    out = out.astype(BF)
    for i in range(4):
        cols = slice(i * 256, (i + 1) * 256)
        out_ref[i, :128, :] = out[:, cols]
        out_ref[i, 128:160, :] = high[:, cols]
        out_ref[i, 160:192, :] = low[:, cols]
        out_ref[i, 192:208, :] = rest[:, cols]


def merge_kernel(parts, out_ref):
    c = lax.axis_index("c")
    hi = lax.Precision.HIGHEST
    ends = [parts[i, 192:208, :].astype(F32) for i in range(4)]
    tops = [e[0:1] + e[1:2] + e[2:3] for e in ends]
    top = jnp.maximum(jnp.maximum(tops[0], tops[1]), jnp.maximum(tops[2], tops[3]))
    factors = [jnp.exp2(t - top) for t in tops]
    total = sum(f * (e[3:4] + e[4:5] + e[5:6]) for f, e in zip(factors, ends))
    shares = [f / total for f in factors]
    out = sum(s * parts[i, :128, :].astype(F32) for i, s in enumerate(shares))
    att = out.T.astype(BF)
    mass = jnp.concatenate(
        [s * (parts[i, 128:160, :].astype(F32) + parts[i, 160:192, :].astype(F32)) for i, s in enumerate(shares)], axis=0
    )
    i = lax.broadcasted_iota(jnp.int32, (128, 128), 0)
    b = lax.broadcasted_iota(jnp.int32, (128, 128), 1)
    cc = jnp.bitwise_xor((i >> 4) & 1, c)
    place = ((i >> 1) & 1) * 64 + ((i >> 2) & 3) * 16 + (i >> 5) * 4 + cc * 2 + (i & 1)
    order = (place == b).astype(F32)
    r = lax.broadcasted_iota(jnp.int32, (16, 256), 0)
    t = lax.broadcasted_iota(jnp.int32, (16, 256), 1)
    row = lax.broadcasted_iota(jnp.int32, (16, 128), 0)
    pick = ((r < 12) & ((t >> 6) == (r & 3))).astype(F32)
    m = jnp.dot(nt(pick, mass, hi), order, preferred_element_type=F32, precision=hi)
    a, d, e = thirds(m)
    packed = jnp.where(row < 4, a, jnp.where(row < 8, d, jnp.where(row < 12, e, 0.0))).astype(BF)
    out_ref[:256, :] = att
    out_ref[256:272, :] = packed


def finish_kernel(att, rows, oown, ooth, bias, gate, out_ref, mass_ref):
    zh, c, w = (lax.axis_index(n) for n in ("zh", "c", "w"))
    a = jnp.concatenate([att[y, i] for y in range(4) for i in range(4)], axis=1)
    weights = []
    for x in range(4):
        both = []
        for ref in (oown, ooth):
            piece = []
            for y in range(4):
                for ww in range(2):
                    slot = jnp.where(zh == 0, ww, 1 - ww)
                    for j in range(2):
                        start = pl.multiple_of(256 + y * 192 + slot * 96 + j * 48, 16)
                        piece.append(ref[x, pl.ds(start, 48), :])
            both.append(jnp.concatenate(piece, axis=1))
        weights.append(jnp.where(c == 0, both[0], both[1]))
        weights.append(jnp.where(c == 0, both[1], both[0]))
    total = nt(a, jnp.concatenate(weights, axis=0))
    out_ref[...] = ((total + bias[...]) * gate[...]).astype(BF)
    for j in range(2):
        r = rows[w * 2 + j, 256:272, :].astype(F32)
        lower = r[0:2] + r[4:6] + r[8:10]
        upper = r[2:4] + r[6:8] + r[10:12]
        mass_ref[j] = jnp.where(zh == 0, lower, upper)


def swap(v, axis):
    return lax.ppermute(v, axis, [(0, 1), (1, 0)])


def spread(v, axis):
    wide = jnp.broadcast_to(v[None], (4,) + v.shape)
    return lax.all_to_all(wide, axis, 0, 0, tiled=True)


def turn(v, axis, k):
    return lax.ppermute(v, axis, [(i, (i + k) % 4) for i in range(4)])


def per_device(
    tokens, qkv_weight, qkv_bias, q_gain, k_gain, cache_kv, cache_scale, cache_code, block_mask, out_weight,
    out_bias, out_gate,
):
    sd = jax.ShapeDtypeStruct

    keep, send, kept, sent, first, flip = call(
        prep_kernel,
        [sd((144, 128), BF)] * 2 + [sd((256, 128), BF)] * 2 + [sd((384, 128), BF), sd((96, 128), BF)],
        6,
        [
            pltpu.VMEM((2, 2), F32), pltpu.VMEM((1, 2), jnp.int32), pltpu.VMEM((48, 768), BF),
            pltpu.VMEM((128, 512), BF), pltpu.VMEM((128, 384), BF), pltpu.VMEM((48, 256), BF),
            pltpu.SemaphoreType.DMA((6,)),
        ],
        HB, None, "prep",
    )(cache_scale, cache_code.reshape(1, 2), qkv_weight, cache_kv, tokens, out_weight.T)

    recv = swap(send, "zh")
    flip = lax.ppermute(
        flip, ("zh", "zl", "w", "y"),
        [
            (((zh * 4 + zl) * 2 + w) * 4 + y, ((w * 4 + y) * 2 + zh) * 4 + zl)
            for zh in range(2) for zl in range(4) for w in range(2) for y in range(4)
        ],
    )
    pay, first = lax.optimization_barrier((jnp.concatenate([keep, recv, flip], axis=0), first))
    along = spread(pay, "zl").reshape(4, 384, 128)
    toks = lax.all_gather(first, ("w", "zh"), axis=0, tiled=False)
    along, toks = lax.optimization_barrier((along, toks))
    xs = spread(toks, "y").reshape(4, 4, 384, 128)
    wts = along[:, :288]
    turned = [turn(wts, "x", k) for k in (1, 2, 3)]
    mine = jnp.concatenate([along[:, 288:].reshape(384, 128), sent], axis=0)
    theirs = swap(mine, "zh")
    *turned, theirs, xs = lax.optimization_barrier((*turned, theirs, xs))
    wown = jnp.stack([wts, *turned])
    woth = swap(wown.reshape(16, 288, 128), "c").reshape(4, 4, 2, 144, 128)
    wown = wown.reshape(4, 4, 2, 144, 128)

    q, fresh = call(project_kernel, [sd((4, 1024, 128), BF), sd((512, 128), BF)], 8, limit=24, name="project")(
        xs, wown, woth, qkv_bias[None], q_gain[None], k_gain[None], mine, theirs
    )
    qs = lax.all_to_all(q, "x", 0, 0, tiled=True)
    kv = call(select_kernel, sd((512, 128), BF), 3, limit=24, name="select", cover=30)(fresh, kept, theirs)
    kv0 = lax.all_gather(kv, "zl", axis=0, tiled=False)
    kv0, qs = lax.optimization_barrier((kv0, qs))
    kv1 = swap(kv0, "c")
    ooth = swap(qs, "c")
    kv1, ooth = lax.optimization_barrier((kv1, ooth))

    parts = call(
        attend_kernel, sd((4, 208, 256), BF), 4, [pltpu.VMEM((2048, 1024), F32), pltpu.VMEM((32, 1024), F32)],
        limit=32, name="attend",
    )(qs, kv0, kv1, block_mask)
    parts = lax.all_to_all(parts, "x", 0, 0, tiled=True)
    done = call(merge_kernel, sd((272, 128), BF), 1, limit=16, name="merge")(parts)
    rows = lax.all_gather(done, ("w", "zh"), axis=0, tiled=False)
    att = lax.all_gather(
        lax.dynamic_slice_in_dim(rows, lax.axis_index("zh") * 128, 128, 1), "y", axis=0, tiled=False
    )
    return call(finish_kernel, [sd((128, 384), BF), sd((2, 2, 128), F32)], 6, limit=24, name="finish")(
        att, rows, qs, ooth, out_bias[None], out_gate[None]
    )


def solution(mesh):
    split = Mesh(mesh.devices.reshape(2, 4, 4, 2, 2, 4), ("zh", "zl", "x", "c", "w", "y"))
    seq, head = ("zh", "zl", "x", "c"), ("w", "y")
    in_specs = (
        P(seq, head), P(seq, head), P(head), P(), P(), P(seq, head), P(seq, head), P(seq), P(), P(head, seq),
        P(head), P(head),
    )
    out_specs = (P(seq, head), P(head, seq, None))
    return jax.shard_map(per_device, mesh=split, in_specs=in_specs, out_specs=out_specs, check_vma=False)
```

```python
import functools
import math

import jax
import jax.numpy as jnp
from jax import lax
from jax.experimental import pallas as pl
from jax.experimental.pallas import tpu as pltpu
from jax.sharding import Mesh, PartitionSpec as P

BF = jnp.bfloat16
F32 = jnp.float32
DH = 128
FRESH = 1e30
FLOOR = -1e29
SHUT = -1e30
LOG2E = 1.4426950408889634

VM = pl.BlockSpec(memory_space=pltpu.VMEM)
HB = pl.BlockSpec(memory_space=pltpu.HBM)


def call(kernel, outs, n_in, scratch=(), place=VM, limit=48, name=None, cover=0, first=VM):
    multiple = isinstance(outs, (list, tuple))
    cost = pl.CostEstimate(flops=cover * 10**9, bytes_accessed=0, transcendentals=0) if cover else None
    return pl.pallas_call(
        kernel,
        out_shape=outs,
        in_specs=[place] * n_in,
        out_specs=[first] + [VM] * (len(outs) - 1) if multiple else VM,
        scratch_shapes=list(scratch),
        compiler_params=pltpu.CompilerParams(vmem_limit_bytes=limit * 1024 * 1024 if limit else None),
        cost_estimate=cost,
        name=name,
    )


def nt(a, b, precision=None):
    return lax.dot_general(
        a, b, (((1,), (1,)), ((), ())), preferred_element_type=F32, precision=precision
    )


def tn(a, b):
    return lax.dot_general(a, b, (((0,), (0,)), ((), ())), preferred_element_type=F32)


def prep_kernel(
    scale_h, code_h, w_h, cache_h, tok_h, ot_h, keep_ref, send_ref, kept_ref, sent_ref, first_ref, flip_ref, scale, code,
    w_ref, cache_ref, tok_ref, ot_ref, sems
):
    zh = lax.axis_index("zh")
    pairs = ((w_h, w_ref), (cache_h, cache_ref), (scale_h, scale), (code_h, code), (tok_h, tok_ref), (ot_h, ot_ref))
    copies = [pltpu.make_async_copy(src, dst, sems.at[i]) for i, (src, dst) in enumerate(pairs)]
    for copy in copies:
        copy.start()
    for copy in copies:
        copy.wait()
    for t in range(3):
        a = w_ref[:, t * 128 : (t + 1) * 128]
        b = w_ref[:, 384 + t * 128 : 384 + (t + 1) * 128]
        keep_ref[t * 48 : (t + 1) * 48, :] = jnp.where(zh == 0, a, b)
        send_ref[t * 48 : (t + 1) * 48, :] = jnp.where(zh == 0, b, a)
    for part in range(2):
        for blk in range(2):
            rows = slice(blk * 64, blk * 64 + 64)
            at = slice(part * 128 + blk * 64, part * 128 + blk * 64 + 64)
            cached = jnp.broadcast_to(code[0:1, blk : blk + 1], (64, 128)) == 1
            both = []
            for j in range(2):
                raw = cache_ref[rows, j * 256 + part * 128 : j * 256 + part * 128 + 128]
                factor = jnp.broadcast_to(scale[blk : blk + 1, j : j + 1], (64, 128))
                both.append(jnp.where(cached, raw.astype(F32) * factor, FRESH).astype(BF))
            kept_ref[at, :] = jnp.where(zh == 0, both[0], both[1])
            sent_ref[at, :] = jnp.where(zh == 0, both[1], both[0])
    for f in range(3):
        first_ref[f * 128 : (f + 1) * 128, :] = tok_ref[:, f * 128 : (f + 1) * 128]
    for j in range(2):
        flip_ref[j * 48 : (j + 1) * 48, :] = ot_ref[:, j * 128 : (j + 1) * 128]


def bias_kernel(bias, out_ref):
    out_ref[...] = jnp.where(lax.axis_index("zh") == 0, bias[:, :384], bias[:, 384:])


def projected(xs, wown, woth):
    zh, x0, c = (lax.axis_index(n) for n in ("zh", "x", "c"))
    total = jnp.zeros((256, 384), F32)
    for yy in range(4):
        for w in range(2):
            slot = jnp.where(zh == 0, w, 1 - w)
            rows = []
            for z in range(2):
                tiles = [xs[yy, w * 2 + z, f * 128 : (f + 1) * 128, :] for f in range(3)]
                rows.append(jnp.concatenate(tiles, axis=1))
            x = jnp.concatenate(rows, axis=0)
            pieces = []
            for xx in range(4):
                k = (x0 - xx) & 3
                own = jnp.concatenate([wown[k, yy, slot, t * 48 : (t + 1) * 48, :] for t in range(3)], axis=1)
                oth = jnp.concatenate([woth[k, yy, slot, t * 48 : (t + 1) * 48, :] for t in range(3)], axis=1)
                pieces.append(jnp.where(c == 0, own, oth))
                pieces.append(jnp.where(c == 0, oth, own))
            total = total + jnp.dot(x, jnp.concatenate(pieces, axis=0), preferred_element_type=F32)
    return total


def scaled(v, gain):
    ms = jnp.mean(v * v, axis=-1, keepdims=True)
    return (v * lax.rsqrt(ms + 1e-06) * gain).astype(BF)


def project_kernel(xs, wown, woth, bias, qg, kg, mine, theirs, out_ref, kv_ref, tile, sems):
    total = projected(xs, wown, woth) + bias[...]
    tile[:256, :] = scaled(total[:, :128], qg[...])
    for z in range(4):
        tile[256 + z * 192 : 352 + z * 192, :] = mine[z * 96 : (z + 1) * 96, :]
        tile[352 + z * 192 : 448 + z * 192, :] = theirs[z * 96 : (z + 1) * 96, :]
    copies = [pltpu.make_async_copy(tile, out_ref.at[i], sems.at[i]) for i in range(4)]
    for copy in copies:
        copy.start()
    kv_ref[:256, :] = scaled(total[:, 128:256], kg[...])
    kv_ref[256:, :] = total[:, 256:].astype(BF)
    for copy in copies:
        copy.wait()


def select_kernel(fresh, kept, theirs, kv_ref):
    zh = lax.axis_index("zh")
    for part in range(2):
        a = kept[part * 128 : part * 128 + 128, :]
        b = theirs[384 + part * 128 : 384 + part * 128 + 128, :]
        for z in range(2):
            rows = slice(part * 256 + z * 128, part * 256 + (z + 1) * 128)
            cached = jnp.where(zh == z, a, b)
            kv_ref[rows, :] = jnp.where(cached.astype(F32) < 1e29, cached, fresh[rows, :])


def thirds(v):
    a = v.astype(BF).astype(F32)
    b = (v - a).astype(BF).astype(F32)
    return a, b, v - a - b


def attend_kernel(q_ref, kv0, kv1, bm_ref, out_ref, s_ref, mask_ref):
    unit = LOG2E / math.sqrt(DH)
    zl, x, c = (lax.axis_index(n) for n in ("zl", "x", "c"))
    r = lax.broadcasted_iota(jnp.int32, (32, 128), 0)
    b = lax.broadcasted_iota(jnp.int32, (32, 128), 1)
    cc = jnp.bitwise_xor(r >> 4, c)
    keys = ((r >> 1) & 1) * 64 + ((r >> 2) & 3) * 16 + x * 4 + cc * 2 + (r & 1)
    picked = nt((keys == b).astype(BF), bm_ref[...].astype(F32).astype(BF))
    a = lax.broadcasted_iota(jnp.int32, (128, 1024), 0)
    t = lax.broadcasted_iota(jnp.int32, (128, 1024), 1)
    rows = ((t >> 7) & 1) * 64 + zl * 16 + (t >> 8) * 4 + c * 2 + ((t >> 6) & 1)
    mask_ref[...] = jnp.dot(picked.astype(BF), (rows == a).astype(BF), preferred_element_type=F32)
    q = jnp.concatenate([q_ref[i, :256, :] for i in range(4)], axis=0)
    top = jnp.full((1, 1024), FLOOR, F32)
    for ch in range(8):
        kv = (kv0, kv1)[ch // 4]
        s = nt(kv[ch % 4, :256, :], q) * unit
        for b in range(4):
            row = ch * 4 + b
            open_ = mask_ref[row : row + 1, :] > 0.5
            sb = jnp.where(open_, s[b * 64 : (b + 1) * 64], SHUT)
            s_ref[ch * 256 + b * 64 : ch * 256 + (b + 1) * 64, :] = sb
            top = jnp.maximum(top, jnp.max(sb, axis=0, keepdims=True))
    total = jnp.zeros((1, 1024), F32)
    out = jnp.zeros((128, 1024), F32)
    mass = []
    for ch in range(8):
        kv = (kv0, kv1)[ch // 4]
        p = jnp.exp2(s_ref[ch * 256 : (ch + 1) * 256, :] - top)
        for b in range(4):
            row = jnp.sum(p[b * 64 : (b + 1) * 64], axis=0, keepdims=True)
            mass.append(row)
            total = total + row
        out = out + tn(kv[ch % 4, 256:, :], p.astype(BF))
    sums = jnp.concatenate(mass, axis=0)
    high = sums.astype(BF)
    low = (sums - high.astype(F32)).astype(BF)
    rest = jnp.concatenate([*thirds(top), *thirds(total), jnp.zeros((10, 1024), F32)], axis=0).astype(BF)
    out = out.astype(BF)
    for i in range(4):
        cols = slice(i * 256, (i + 1) * 256)
        out_ref[i, :128, :] = out[:, cols]
        out_ref[i, 128:160, :] = high[:, cols]
        out_ref[i, 160:192, :] = low[:, cols]
        out_ref[i, 192:208, :] = rest[:, cols]


def merge_kernel(parts, out_ref):
    c = lax.axis_index("c")
    hi = lax.Precision.HIGHEST
    ends = [parts[i, 192:208, :].astype(F32) for i in range(4)]
    tops = [e[0:1] + e[1:2] + e[2:3] for e in ends]
    top = jnp.maximum(jnp.maximum(tops[0], tops[1]), jnp.maximum(tops[2], tops[3]))
    factors = [jnp.exp2(t - top) for t in tops]
    total = sum(f * (e[3:4] + e[4:5] + e[5:6]) for f, e in zip(factors, ends))
    shares = [f / total for f in factors]
    out = sum(s * parts[i, :128, :].astype(F32) for i, s in enumerate(shares))
    att = out.T.astype(BF)
    mass = jnp.concatenate(
        [s * (parts[i, 128:160, :].astype(F32) + parts[i, 160:192, :].astype(F32)) for i, s in enumerate(shares)], axis=0
    )
    i = lax.broadcasted_iota(jnp.int32, (128, 128), 0)
    b = lax.broadcasted_iota(jnp.int32, (128, 128), 1)
    cc = jnp.bitwise_xor((i >> 4) & 1, c)
    place = ((i >> 1) & 1) * 64 + ((i >> 2) & 3) * 16 + (i >> 5) * 4 + cc * 2 + (i & 1)
    order = (place == b).astype(F32)
    r = lax.broadcasted_iota(jnp.int32, (16, 256), 0)
    t = lax.broadcasted_iota(jnp.int32, (16, 256), 1)
    row = lax.broadcasted_iota(jnp.int32, (16, 128), 0)
    pick = ((r < 12) & ((t >> 6) == (r & 3))).astype(F32)
    m = jnp.dot(nt(pick, mass, hi), order, preferred_element_type=F32, precision=hi)
    a, d, e = thirds(m)
    packed = jnp.where(row < 4, a, jnp.where(row < 8, d, jnp.where(row < 12, e, 0.0))).astype(BF)
    out_ref[:256, :] = att
    out_ref[256:272, :] = packed


def finish_kernel(att, rows, oown, ooth, bias, gate, out_ref, mass_ref):
    zh, c, w = (lax.axis_index(n) for n in ("zh", "c", "w"))
    a = jnp.concatenate([att[y, i] for y in range(4) for i in range(4)], axis=1)
    weights = []
    for x in range(4):
        both = []
        for ref in (oown, ooth):
            piece = []
            for y in range(4):
                for ww in range(2):
                    slot = jnp.where(zh == 0, ww, 1 - ww)
                    for j in range(2):
                        start = pl.multiple_of(256 + y * 192 + slot * 96 + j * 48, 16)
                        piece.append(ref[x, pl.ds(start, 48), :])
            both.append(jnp.concatenate(piece, axis=1))
        weights.append(jnp.where(c == 0, both[0], both[1]))
        weights.append(jnp.where(c == 0, both[1], both[0]))
    total = nt(a, jnp.concatenate(weights, axis=0))
    out_ref[...] = ((total + bias[...]) * gate[...]).astype(BF)
    for j in range(2):
        r = rows[w * 2 + j, 256:272, :].astype(F32)
        lower = r[0:2] + r[4:6] + r[8:10]
        upper = r[2:4] + r[6:8] + r[10:12]
        mass_ref[j] = jnp.where(zh == 0, lower, upper)


def swap(v, axis):
    return lax.ppermute(v, axis, [(0, 1), (1, 0)])


def spread(v, axis):
    wide = jnp.broadcast_to(v[None], (4,) + v.shape)
    return lax.all_to_all(wide, axis, 0, 0, tiled=True)


def turn(v, axis, k):
    return lax.ppermute(v, axis, [(i, (i + k) % 4) for i in range(4)])


def per_device(
    tokens, qkv_weight, qkv_bias, q_gain, k_gain, cache_kv, cache_scale, cache_code, block_mask, out_weight,
    out_bias, out_gate,
):
    sd = jax.ShapeDtypeStruct

    keep, send, kept, sent, first, flip = call(
        prep_kernel,
        [sd((144, 128), BF)] * 2 + [sd((256, 128), BF)] * 2 + [sd((384, 128), BF), sd((96, 128), BF)],
        6,
        [
            pltpu.VMEM((2, 2), F32), pltpu.VMEM((1, 2), jnp.int32), pltpu.VMEM((48, 768), BF),
            pltpu.VMEM((128, 512), BF), pltpu.VMEM((128, 384), BF), pltpu.VMEM((48, 256), BF),
            pltpu.SemaphoreType.DMA((6,)),
        ],
        HB, None, "prep",
    )(cache_scale, cache_code.reshape(1, 2), qkv_weight, cache_kv, tokens, out_weight.T)

    recv = swap(send, "zh")
    flip = lax.ppermute(
        flip, ("zh", "zl", "w", "y"),
        [
            (((zh * 4 + zl) * 2 + w) * 4 + y, ((w * 4 + y) * 2 + zh) * 4 + zl)
            for zh in range(2) for zl in range(4) for w in range(2) for y in range(4)
        ],
    )
    pay, first = lax.optimization_barrier((jnp.concatenate([keep, recv, flip], axis=0), first))
    along = spread(pay, "zl").reshape(4, 384, 128)
    toks = lax.all_gather(first, ("w", "zh"), axis=0, tiled=False)
    along, toks = lax.optimization_barrier((along, toks))
    xs = spread(toks, "y").reshape(4, 4, 384, 128)
    wts = along[:, :288]
    turned = [turn(wts, "x", k) for k in (1, 2, 3)]
    mine = jnp.concatenate([along[:, 288:].reshape(384, 128), sent], axis=0)
    theirs = swap(mine, "zh")
    wown = jnp.stack([wts, *turned])
    woth = swap(wown.reshape(16, 288, 128), "c").reshape(4, 4, 2, 144, 128)
    xs, theirs, bias = lax.optimization_barrier((xs, theirs, qkv_bias[None]))
    bias = call(bias_kernel, sd((1, 384), F32), 1, limit=16, name="bias", cover=40)(bias)
    xs, theirs, bias = lax.optimization_barrier((xs, theirs, bias))
    wown = wown.reshape(4, 4, 2, 144, 128)

    q, fresh = call(project_kernel, [sd((4, 1024, 128), BF), sd((512, 128), BF)], 8,
        [pltpu.VMEM((1024, 128), BF), pltpu.SemaphoreType.DMA((4,))], limit=24, name="project", first=HB,
    )(
        xs, wown, woth, bias, q_gain[None], k_gain[None], mine, theirs
    )
    qs = lax.all_to_all(q, "x", 0, 0, tiled=True)
    kv = call(select_kernel, sd((512, 128), BF), 3, limit=24, name="select", cover=30)(fresh, kept, theirs)
    kv0 = lax.all_gather(kv, "zl", axis=0, tiled=False)
    kv0, qs = lax.optimization_barrier((kv0, qs))
    kv1 = swap(kv0, "c")
    ooth = swap(qs, "c")
    kv1, ooth = lax.optimization_barrier((kv1, ooth))

    parts = call(
        attend_kernel, sd((4, 208, 256), BF), 4, [pltpu.VMEM((2048, 1024), F32), pltpu.VMEM((32, 1024), F32)],
        limit=32, name="attend",
    )(qs, kv0, kv1, block_mask)
    parts = lax.all_to_all(parts, "x", 0, 0, tiled=True)
    done = call(merge_kernel, sd((272, 128), BF), 1, limit=16, name="merge")(parts)
    rows = lax.all_gather(done, ("w", "zh"), axis=0, tiled=False)
    att = lax.all_gather(
        lax.dynamic_slice_in_dim(rows, lax.axis_index("zh") * 128, 128, 1), "y", axis=0, tiled=False
    )
    return call(finish_kernel, [sd((128, 384), BF), sd((2, 2, 128), F32)], 6, limit=24, name="finish")(
        att, rows, qs, ooth, out_bias[None], out_gate[None]
    )


def solution(mesh):
    split = Mesh(mesh.devices.reshape(2, 4, 4, 2, 2, 4), ("zh", "zl", "x", "c", "w", "y"))
    seq, head = ("zh", "zl", "x", "c"), ("w", "y")
    in_specs = (
        P(seq, head), P(seq, head), P(head), P(), P(), P(seq, head), P(seq, head), P(seq), P(), P(head, seq),
        P(head), P(head),
    )
    out_specs = (P(seq, head), P(head, seq, None))
    return jax.shard_map(per_device, mesh=split, in_specs=in_specs, out_specs=out_specs, check_vma=False)
```

```python
import functools
import math

import jax
import jax.numpy as jnp
from jax import lax
from jax.experimental import pallas as pl
from jax.experimental.pallas import tpu as pltpu
from jax.sharding import Mesh, PartitionSpec as P

BF = jnp.bfloat16
F32 = jnp.float32
DH = 128
FRESH = 1e30
FLOOR = -1e29
SHUT = -1e30
LOG2E = 1.4426950408889634

VM = pl.BlockSpec(memory_space=pltpu.VMEM)
HB = pl.BlockSpec(memory_space=pltpu.HBM)


def call(kernel, outs, n_in, scratch=(), place=VM, limit=48, name=None, cover=0, first=VM):
    multiple = isinstance(outs, (list, tuple))
    cost = pl.CostEstimate(flops=cover * 10**9, bytes_accessed=0, transcendentals=0) if cover else None
    return pl.pallas_call(
        kernel,
        out_shape=outs,
        in_specs=[place] * n_in,
        out_specs=[first] + [VM] * (len(outs) - 1) if multiple else VM,
        scratch_shapes=list(scratch),
        compiler_params=pltpu.CompilerParams(vmem_limit_bytes=limit * 1024 * 1024 if limit else None),
        cost_estimate=cost,
        name=name,
    )


def nt(a, b, precision=None):
    return lax.dot_general(
        a, b, (((1,), (1,)), ((), ())), preferred_element_type=F32, precision=precision
    )


def tn(a, b):
    return lax.dot_general(a, b, (((0,), (0,)), ((), ())), preferred_element_type=F32)


def prep_kernel(
    scale_h, code_h, w_h, cache_h, tok_h, ot_h, keep_ref, send_ref, kept_ref, sent_ref, first_ref, flip_ref, scale, code,
    w_ref, cache_ref, tok_ref, ot_ref, sems
):
    zh = lax.axis_index("zh")
    pairs = ((w_h, w_ref), (cache_h, cache_ref), (scale_h, scale), (code_h, code), (tok_h, tok_ref), (ot_h, ot_ref))
    copies = [pltpu.make_async_copy(src, dst, sems.at[i]) for i, (src, dst) in enumerate(pairs)]
    for copy in copies:
        copy.start()
    for copy in copies:
        copy.wait()
    for t in range(3):
        a = w_ref[:, t * 128 : (t + 1) * 128]
        b = w_ref[:, 384 + t * 128 : 384 + (t + 1) * 128]
        keep_ref[t * 48 : (t + 1) * 48, :] = jnp.where(zh == 0, a, b)
        send_ref[t * 48 : (t + 1) * 48, :] = jnp.where(zh == 0, b, a)
    for part in range(2):
        for blk in range(2):
            rows = slice(blk * 64, blk * 64 + 64)
            at = slice(part * 128 + blk * 64, part * 128 + blk * 64 + 64)
            cached = jnp.broadcast_to(code[0:1, blk : blk + 1], (64, 128)) == 1
            both = []
            for j in range(2):
                raw = cache_ref[rows, j * 256 + part * 128 : j * 256 + part * 128 + 128]
                factor = jnp.broadcast_to(scale[blk : blk + 1, j : j + 1], (64, 128))
                both.append(jnp.where(cached, raw.astype(F32) * factor, FRESH).astype(BF))
            kept_ref[at, :] = jnp.where(zh == 0, both[0], both[1])
            sent_ref[at, :] = jnp.where(zh == 0, both[1], both[0])
    for f in range(3):
        first_ref[f * 128 : (f + 1) * 128, :] = tok_ref[:, f * 128 : (f + 1) * 128]
    for j in range(2):
        flip_ref[j * 48 : (j + 1) * 48, :] = ot_ref[:, j * 128 : (j + 1) * 128]


def bias_kernel(bias, out_ref):
    out_ref[...] = jnp.where(lax.axis_index("zh") == 0, bias[:, :384], bias[:, 384:])


def projected(xs, wown, woth):
    zh, x0, c = (lax.axis_index(n) for n in ("zh", "x", "c"))
    total = jnp.zeros((256, 384), F32)
    for yy in range(4):
        for w in range(2):
            slot = jnp.where(zh == 0, w, 1 - w)
            rows = []
            for z in range(2):
                tiles = [xs[yy, w * 2 + z, f * 128 : (f + 1) * 128, :] for f in range(3)]
                rows.append(jnp.concatenate(tiles, axis=1))
            x = jnp.concatenate(rows, axis=0)
            pieces = []
            for xx in range(4):
                k = (x0 - xx) & 3
                own = jnp.concatenate([wown[k, yy, slot, t * 48 : (t + 1) * 48, :] for t in range(3)], axis=1)
                oth = jnp.concatenate([woth[k, yy, slot, t * 48 : (t + 1) * 48, :] for t in range(3)], axis=1)
                pieces.append(jnp.where(c == 0, own, oth))
                pieces.append(jnp.where(c == 0, oth, own))
            total = total + jnp.dot(x, jnp.concatenate(pieces, axis=0), preferred_element_type=F32)
    return total


def scaled(v, gain):
    ms = jnp.mean(v * v, axis=-1, keepdims=True)
    return (v * lax.rsqrt(ms + 1e-06) * gain).astype(BF)


def project_kernel(xs, wown, woth, bias, qg, kg, mine, theirs, out_ref, kv_ref, tile, sems):
    total = projected(xs, wown, woth) + bias[...]
    tile[:256, :] = scaled(total[:, :128], qg[...])
    for z in range(4):
        tile[256 + z * 192 : 352 + z * 192, :] = mine[z * 96 : (z + 1) * 96, :]
        tile[352 + z * 192 : 448 + z * 192, :] = theirs[z * 96 : (z + 1) * 96, :]
    copies = [pltpu.make_async_copy(tile, out_ref.at[i], sems.at[i]) for i in range(4)]
    for copy in copies:
        copy.start()
    kv_ref[:256, :] = scaled(total[:, 128:256], kg[...])
    kv_ref[256:, :] = total[:, 256:].astype(BF)
    for copy in copies:
        copy.wait()


def select_kernel(fresh, kept, theirs, kv_ref):
    zh = lax.axis_index("zh")
    for part in range(2):
        a = kept[part * 128 : part * 128 + 128, :]
        b = theirs[384 + part * 128 : 384 + part * 128 + 128, :]
        for z in range(2):
            rows = slice(part * 256 + z * 128, part * 256 + (z + 1) * 128)
            cached = jnp.where(zh == z, a, b)
            kv_ref[rows, :] = jnp.where(cached.astype(F32) < 1e29, cached, fresh[rows, :])


def thirds(v):
    a = v.astype(BF).astype(F32)
    b = (v - a).astype(BF).astype(F32)
    return a, b, v - a - b


def attend_kernel(q_ref, kv0, kv1, bm_ref, out_ref, s_ref, mask_ref):
    unit = LOG2E / math.sqrt(DH)
    zl, x, c = (lax.axis_index(n) for n in ("zl", "x", "c"))
    r = lax.broadcasted_iota(jnp.int32, (32, 128), 0)
    b = lax.broadcasted_iota(jnp.int32, (32, 128), 1)
    cc = jnp.bitwise_xor(r >> 4, c)
    keys = ((r >> 1) & 1) * 64 + ((r >> 2) & 3) * 16 + x * 4 + cc * 2 + (r & 1)
    picked = nt((keys == b).astype(BF), bm_ref[...].astype(F32).astype(BF))
    a = lax.broadcasted_iota(jnp.int32, (128, 1024), 0)
    t = lax.broadcasted_iota(jnp.int32, (128, 1024), 1)
    rows = ((t >> 7) & 1) * 64 + zl * 16 + (t >> 8) * 4 + c * 2 + ((t >> 6) & 1)
    mask_ref[...] = jnp.dot(picked.astype(BF), (rows == a).astype(BF), preferred_element_type=F32)
    q = jnp.concatenate([q_ref[i, :256, :] for i in range(4)], axis=0)
    top = jnp.full((1, 1024), FLOOR, F32)
    for ch in range(8):
        kv = (kv0, kv1)[ch // 4]
        s = nt(kv[ch % 4, :256, :], q) * unit
        for b in range(4):
            row = ch * 4 + b
            open_ = mask_ref[row : row + 1, :] > 0.5
            sb = jnp.where(open_, s[b * 64 : (b + 1) * 64], SHUT)
            s_ref[ch * 256 + b * 64 : ch * 256 + (b + 1) * 64, :] = sb
            top = jnp.maximum(top, jnp.max(sb, axis=0, keepdims=True))
    total = jnp.zeros((1, 1024), F32)
    out = jnp.zeros((128, 1024), F32)
    mass = []
    for ch in range(8):
        kv = (kv0, kv1)[ch // 4]
        p = jnp.exp2(s_ref[ch * 256 : (ch + 1) * 256, :] - top)
        for b in range(4):
            row = jnp.sum(p[b * 64 : (b + 1) * 64], axis=0, keepdims=True)
            mass.append(row)
            total = total + row
        out = out + tn(kv[ch % 4, 256:, :], p.astype(BF))
    sums = jnp.concatenate(mass, axis=0)
    high = sums.astype(BF)
    rest = jnp.concatenate([*thirds(top), *thirds(total), jnp.zeros((10, 1024), F32)], axis=0).astype(BF)
    out = out.astype(BF)
    for i in range(4):
        cols = slice(i * 256, (i + 1) * 256)
        out_ref[i, :128, :] = out[:, cols]
        out_ref[i, 128:160, :] = high[:, cols]
        out_ref[i, 160:176, :] = rest[:, cols]


def merge_kernel(parts, out_ref):
    c = lax.axis_index("c")
    hi = lax.Precision.HIGHEST
    ends = [parts[i, 160:176, :].astype(F32) for i in range(4)]
    tops = [e[0:1] + e[1:2] + e[2:3] for e in ends]
    top = jnp.maximum(jnp.maximum(tops[0], tops[1]), jnp.maximum(tops[2], tops[3]))
    factors = [jnp.exp2(t - top) for t in tops]
    total = sum(f * (e[3:4] + e[4:5] + e[5:6]) for f, e in zip(factors, ends))
    shares = [f / total for f in factors]
    out = sum(s * parts[i, :128, :].astype(F32) for i, s in enumerate(shares))
    att = out.T.astype(BF)
    mass = jnp.concatenate(
        [s * parts[i, 128:160, :].astype(F32) for i, s in enumerate(shares)], axis=0
    )
    i = lax.broadcasted_iota(jnp.int32, (128, 128), 0)
    b = lax.broadcasted_iota(jnp.int32, (128, 128), 1)
    cc = jnp.bitwise_xor((i >> 4) & 1, c)
    place = ((i >> 1) & 1) * 64 + ((i >> 2) & 3) * 16 + (i >> 5) * 4 + cc * 2 + (i & 1)
    order = (place == b).astype(F32)
    r = lax.broadcasted_iota(jnp.int32, (16, 256), 0)
    t = lax.broadcasted_iota(jnp.int32, (16, 256), 1)
    row = lax.broadcasted_iota(jnp.int32, (16, 128), 0)
    pick = ((r < 12) & ((t >> 6) == (r & 3))).astype(F32)
    m = jnp.dot(nt(pick, mass, hi), order, preferred_element_type=F32, precision=hi)
    a, d, e = thirds(m)
    packed = jnp.where(row < 4, a, jnp.where(row < 8, d, jnp.where(row < 12, e, 0.0))).astype(BF)
    out_ref[:256, :] = att
    out_ref[256:272, :] = packed


def finish_kernel(att, rows, oown, ooth, bias, gate, out_ref, mass_ref):
    zh, c, w = (lax.axis_index(n) for n in ("zh", "c", "w"))
    a = jnp.concatenate([att[y, i] for y in range(4) for i in range(4)], axis=1)
    weights = []
    for x in range(4):
        both = []
        for ref in (oown, ooth):
            piece = []
            for y in range(4):
                for ww in range(2):
                    slot = jnp.where(zh == 0, ww, 1 - ww)
                    for j in range(2):
                        start = pl.multiple_of(256 + y * 192 + slot * 96 + j * 48, 16)
                        piece.append(ref[x, pl.ds(start, 48), :])
            both.append(jnp.concatenate(piece, axis=1))
        weights.append(jnp.where(c == 0, both[0], both[1]))
        weights.append(jnp.where(c == 0, both[1], both[0]))
    total = nt(a, jnp.concatenate(weights, axis=0))
    out_ref[...] = ((total + bias[...]) * gate[...]).astype(BF)
    for j in range(2):
        r = rows[w * 2 + j, 256:272, :].astype(F32)
        lower = r[0:2] + r[4:6] + r[8:10]
        upper = r[2:4] + r[6:8] + r[10:12]
        mass_ref[j] = jnp.where(zh == 0, lower, upper)


def swap(v, axis):
    return lax.ppermute(v, axis, [(0, 1), (1, 0)])


def spread(v, axis):
    wide = jnp.broadcast_to(v[None], (4,) + v.shape)
    return lax.all_to_all(wide, axis, 0, 0, tiled=True)


def turn(v, axis, k):
    return lax.ppermute(v, axis, [(i, (i + k) % 4) for i in range(4)])


def per_device(
    tokens, qkv_weight, qkv_bias, q_gain, k_gain, cache_kv, cache_scale, cache_code, block_mask, out_weight,
    out_bias, out_gate,
):
    sd = jax.ShapeDtypeStruct

    keep, send, kept, sent, first, flip = call(
        prep_kernel,
        [sd((144, 128), BF)] * 2 + [sd((256, 128), BF)] * 2 + [sd((384, 128), BF), sd((96, 128), BF)],
        6,
        [
            pltpu.VMEM((2, 2), F32), pltpu.VMEM((1, 2), jnp.int32), pltpu.VMEM((48, 768), BF),
            pltpu.VMEM((128, 512), BF), pltpu.VMEM((128, 384), BF), pltpu.VMEM((48, 256), BF),
            pltpu.SemaphoreType.DMA((6,)),
        ],
        HB, None, "prep",
    )(cache_scale, cache_code.reshape(1, 2), qkv_weight, cache_kv, tokens, out_weight.T)

    recv = swap(send, "zh")
    flip = lax.ppermute(
        flip, ("zh", "zl", "w", "y"),
        [
            (((zh * 4 + zl) * 2 + w) * 4 + y, ((w * 4 + y) * 2 + zh) * 4 + zl)
            for zh in range(2) for zl in range(4) for w in range(2) for y in range(4)
        ],
    )
    pay, first = lax.optimization_barrier((jnp.concatenate([keep, recv, flip], axis=0), first))
    along = spread(pay, "zl").reshape(4, 384, 128)
    toks = lax.all_gather(first, ("w", "zh"), axis=0, tiled=False)
    along, toks = lax.optimization_barrier((along, toks))
    xs = spread(toks, "y").reshape(4, 4, 384, 128)
    wts = along[:, :288]
    turned = [turn(wts, "x", k) for k in (1, 2, 3)]
    mine = jnp.concatenate([along[:, 288:].reshape(384, 128), sent], axis=0)
    theirs = swap(mine, "zh")
    wown = jnp.stack([wts, *turned])
    woth = swap(wown.reshape(16, 288, 128), "c").reshape(4, 4, 2, 144, 128)
    xs, theirs, bias = lax.optimization_barrier((xs, theirs, qkv_bias[None]))
    bias = call(bias_kernel, sd((1, 384), F32), 1, limit=16, name="bias", cover=40)(bias)
    xs, theirs, bias = lax.optimization_barrier((xs, theirs, bias))
    wown = wown.reshape(4, 4, 2, 144, 128)

    q, fresh = call(project_kernel, [sd((4, 1024, 128), BF), sd((512, 128), BF)], 8,
        [pltpu.VMEM((1024, 128), BF), pltpu.SemaphoreType.DMA((4,))], limit=24, name="project", first=HB,
    )(
        xs, wown, woth, bias, q_gain[None], k_gain[None], mine, theirs
    )
    qs = lax.all_to_all(q, "x", 0, 0, tiled=True)
    kv = call(select_kernel, sd((512, 128), BF), 3, limit=24, name="select", cover=30)(fresh, kept, theirs)
    kv0 = lax.all_gather(kv, "zl", axis=0, tiled=False)
    kv0, qs = lax.optimization_barrier((kv0, qs))
    kv1 = swap(kv0, "c")
    ooth = swap(qs, "c")
    kv1, ooth = lax.optimization_barrier((kv1, ooth))

    parts = call(
        attend_kernel, sd((4, 176, 256), BF), 4, [pltpu.VMEM((2048, 1024), F32), pltpu.VMEM((32, 1024), F32)],
        limit=32, name="attend",
    )(qs, kv0, kv1, block_mask)
    parts = lax.all_to_all(parts, "x", 0, 0, tiled=True)
    done = call(merge_kernel, sd((272, 128), BF), 1, limit=16, name="merge")(parts)
    rows = lax.all_gather(done, ("w", "zh"), axis=0, tiled=False)
    att = lax.all_gather(
        lax.dynamic_slice_in_dim(rows, lax.axis_index("zh") * 128, 128, 1), "y", axis=0, tiled=False
    )
    return call(finish_kernel, [sd((128, 384), BF), sd((2, 2, 128), F32)], 6, limit=24, name="finish")(
        att, rows, qs, ooth, out_bias[None], out_gate[None]
    )


def solution(mesh):
    split = Mesh(mesh.devices.reshape(2, 4, 4, 2, 2, 4), ("zh", "zl", "x", "c", "w", "y"))
    seq, head = ("zh", "zl", "x", "c"), ("w", "y")
    in_specs = (
        P(seq, head), P(seq, head), P(head), P(), P(), P(seq, head), P(seq, head), P(seq), P(), P(head, seq),
        P(head), P(head),
    )
    out_specs = (P(seq, head), P(head, seq, None))
    return jax.shard_map(per_device, mesh=split, in_specs=in_specs, out_specs=out_specs, check_vma=False)
```
